32 devices in a mesh: fit: 4 (over x, core), row: 8 (over z, y).
Axes of the slice: x: 2, y: 2, z: 4, core: 2. Of those that a mesh axis runs over, the one named last changes fastest.
Arguments:
- factors: bfloat16 [8192, 12, 512], P('row', 'fit'), may hold values from -2 to 2
Outputs:
- exchange: float32 [4, 8192, 2048], P('fit', 'row')
The draws below stay inside these ranges and needn't reach their ends.
All inputs are finite; a program needn't handle non-finite values.
Results may differ from the reference program's by a relative error of at most 0.0003.
Values may be sent and summed in bfloat16 or wider, within the bound.
A program may use at most 192 MiB of HBM per device.

```python
import jax
import jax.numpy as jnp

NBF = 8192
NOCC = 512
NAUX = 12
ROWS = 1024
N_FIT = 4
N_ROW = 8


def steps_of(stream_key, dims, shards, smallest, largest):
    def one(position, parts):
        heights = jax.random.uniform(jax.random.fold_in(jax.random.fold_in(stream_key, 6), position), (parts,), jnp.float32, smallest / len(shards), largest / len(shards))
        return jnp.repeat(jnp.exp(heights), dims[position] // parts).reshape((-1,) + (1,) * (len(dims) - position - 1))

    loudness = one(*shards[0])
    for cut in shards[1:]:
        loudness = loudness * one(*cut)
    return loudness


def gaussian(stream_key, dims, width, bound, shards=(), kind=jnp.bfloat16):
    result = jax.random.normal(stream_key, dims, jnp.float32) * width
    if len(shards) > 0:
        result = steps_of(stream_key, dims, shards, -0.22, 0.18) * result
    return jnp.clip(result, min=-bound, max=bound).astype(kind)


def setup_inputs(seed: int = 0) -> dict:
    arg_keys = jax.random.split(jax.random.key(seed), 2)
    return {
        "factors": gaussian(arg_keys[0], (NBF, NAUX, NOCC), 0.125, 2.0, ((0, 8), (1, 4))),
    }


def reference(factors):
    flat = factors.reshape(NBF, NAUX * NOCC)
    matrix = jnp.dot(flat, flat.T, preferred_element_type=jnp.float32)
    tiled = matrix.reshape(NBF, N_ROW, N_FIT, ROWS // N_FIT)
    return jnp.transpose(tiled, (2, 0, 1, 3)).reshape(N_FIT, NBF, NBF // N_FIT)
```

```python
import jax
import jax.numpy as jnp
from jax import lax
from jax.sharding import PartitionSpec as P


def per_device(factors):
    row_count, local_funcs, occupied = factors.shape
    groups = lax.axis_size("fit")
    blocks = lax.axis_size("row")
    sub_width = row_count // groups
    pieces = factors.reshape(groups, sub_width, local_funcs * occupied)
    mine = lax.all_to_all(pieces, "fit", split_axis=0, concat_axis=0)
    columns = lax.all_gather(mine, "row", axis=0)
    rows = lax.all_gather(factors.reshape(row_count, local_funcs * occupied), "fit", axis=0)
    out = lax.dot_general(
        rows, columns, (((0, 2), (1, 3)), ((), ())), preferred_element_type=jnp.float32
    )
    return out.reshape(1, row_count, blocks * sub_width)


def solution(mesh):
    return jax.shard_map(
        per_device,
        mesh=mesh,
        in_specs=(P("row", "fit", None),),
        out_specs=P("fit", "row", None),
        check_vma=False,
    )
```

```python
import functools

import jax
import jax.numpy as jnp
from jax import lax
from jax.experimental import pallas as pl
from jax.experimental.pallas import tpu as pltpu
from jax.sharding import PartitionSpec as P

MESH = pl.DeviceIdType.MESH
Z_SIZE = 4
Y_SIZE = 2


def gathered_by_collectives(factors):
    row_count, local_funcs, occupied = factors.shape
    groups = lax.axis_size("fit")
    blocks = lax.axis_size("row")
    sub_width = row_count // groups
    pieces = factors.reshape(groups, sub_width, local_funcs * occupied)
    mine = lax.all_to_all(pieces, "fit", split_axis=0, concat_axis=0)
    columns = lax.all_gather(mine, "row", axis=0)
    rows = lax.all_gather(factors.reshape(row_count, local_funcs * occupied), "fit", axis=0)
    out = lax.dot_general(
        rows, columns, (((0, 2), (1, 3)), ((), ())), preferred_element_type=jnp.float32
    )
    return out.reshape(1, row_count, blocks * sub_width)


def kernel(first, a_ref, out_ref, rows, cols, fit_send, fit_recv, send_sem, recv_sem):
    f = lax.axis_index("fit")
    r = lax.axis_index("row")
    z = r // Y_SIZE
    y = r % Y_SIZE
    core_mate = f + 1 - 2 * (f % 2)
    x_peer = (f + 2) % 4
    diagonal = (core_mate + 2) % 4
    subs = (f, core_mate, x_peer, diagonal)
    row_count, width = a_ref.shape
    sub = row_count // 4
    has_up = z < Z_SIZE - 1
    has_down = z > 0
    y_mate = z * Y_SIZE + 1 - y
    parts = [(0, 0, first), (0, first, width - first)] + [(q, 0, width) for q in (1, 2, 3)]

    def row_slice(s):
        return pl.ds(pl.multiple_of(s * sub, sub), sub)

    def greet(fit, row):
        pl.semaphore_signal(
            pltpu.get_barrier_semaphore(), inc=1, device_id=(fit, row), device_id_type=MESH
        )

    greet(core_mate, r)
    greet(x_peer, r)
    greet(f, y_mate)
    pl.when(has_up)(lambda: greet(f, r + Y_SIZE))
    pl.when(has_down)(lambda: greet(f, r - Y_SIZE))
    pl.semaphore_wait(
        pltpu.get_barrier_semaphore(), 3 + has_up.astype(jnp.int32) + has_down.astype(jnp.int32)
    )

    def fit_copy(q, j):
        if q == 2:
            target, s = x_peer, subs[2 ^ j]
        else:
            target, s = core_mate, subs[1 ^ j]
        source = rows.at[1, row_slice(s)] if q == 3 else a_ref.at[row_slice(s)]
        return pltpu.make_async_remote_copy(
            src_ref=source,
            dst_ref=rows.at[q - 1, row_slice(s)],
            send_sem=fit_send.at[q - 1, j],
            recv_sem=fit_recv.at[q - 1, j],
            device_id=(target, r),
            device_id_type=MESH,
        )

    def fit_wait(q, j):
        landed = rows.at[q - 1, row_slice(subs[j])]
        pltpu.make_async_remote_copy(
            src_ref=landed,
            dst_ref=landed,
            send_sem=fit_send.at[q - 1, j],
            recv_sem=fit_recv.at[q - 1, j],
            device_id=(core_mate, r),
            device_id_type=MESH,
        ).wait_recv()

    def slot_of(block, part):
        q, begin, size = parts[part]
        return cols.at[block, q, :, pl.ds(begin, size)]

    def own_source(part):
        q, begin, size = parts[part]
        if q == 0:
            return a_ref.at[row_slice(f), pl.ds(begin, size)]
        return rows.at[q - 1, row_slice(f), pl.ds(begin, size)]

    def plane_copy(direction, block, part, source=None):
        target = (r + Y_SIZE, r - Y_SIZE, y_mate)[direction]
        slot = slot_of(block, part)
        return pltpu.make_async_remote_copy(
            src_ref=slot if source is None else source,
            dst_ref=slot,
            send_sem=send_sem.at[direction, block, part],
            recv_sem=recv_sem.at[block, part],
            device_id=(f, target),
            device_id_type=MESH,
        )

    def plane_wait(block, part):
        plane_copy(2, block, part).wait_recv()

    def send_own(part):
        source = own_source(part)
        pl.when(has_up)(lambda: plane_copy(0, r, part, source).start())
        pl.when(has_down)(lambda: plane_copy(1, r, part, source).start())
        plane_copy(2, r, part, source).start()

    fit_copy(2, 0).start()
    fit_copy(1, 0).start()
    send_own(0)
    send_own(1)
    fit_copy(2, 1).start()
    for j in (1, 2, 3):
        fit_copy(1, j).start()
    fit_wait(1, 0)
    send_own(2)
    plane_wait(y_mate, 0)
    pl.when(has_up)(lambda: plane_copy(0, y_mate, 0).start())
    pl.when(has_down)(lambda: plane_copy(1, y_mate, 0).start())
    fit_wait(2, 0)
    send_own(3)
    fit_copy(2, 2).start()
    fit_wait(2, 1)
    fit_copy(3, 0).start()
    fit_copy(2, 3).start()
    fit_copy(3, 1).start()
    fit_wait(3, 0)
    send_own(4)

    dims = (((1,), (1,)), ((), ()))

    def multiply(operand, block):
        tile = min(512, row_count)

        @pl.loop(0, row_count // tile)
        def _(i):
            here = pl.ds(pl.multiple_of(i * tile, tile), tile)
            total = lax.dot_general(
                a_ref[here, :], operand(0), dims, preferred_element_type=jnp.float32
            )
            for q in (1, 2, 3):
                total += lax.dot_general(
                    rows[q - 1, here, :], operand(q), dims, preferred_element_type=jnp.float32
                )
            out_ref[here, pl.ds(pl.multiple_of(block * sub, sub), sub)] = total

    def finish_fit():
        for j in (2, 3):
            fit_wait(2, j)
            fit_copy(3, j ^ 1).start()
        for j in (1, 2, 3):
            fit_wait(1, j)
            fit_wait(3, j)
        multiply(
            lambda q: a_ref[row_slice(f), :] if q == 0 else rows[q - 1, row_slice(f), :], r
        )

    def stage(d, carry):
        for part, mate in [(0, 0), (0, 1), (1, 0), (2, 0), (3, 0), (4, 0)]:
            line = y if mate == 0 else 1 - y
            for side in (0, 1):
                far = z - d if side == 0 else z + d
                block = far * Y_SIZE + line

                @pl.when((far >= 0) if side == 0 else (far < Z_SIZE))
                def _(block=block, part=part, side=side):
                    plane_wait(block, part)
                    onward = has_up if side == 0 else has_down
                    pl.when(onward)(lambda: plane_copy(side, block, part).start())
                    if part > 0:
                        plane_copy(2, block, part).start()

        pl.when(d == 1)(finish_fit)

        def one_block(t, carry):
            side = t % 2
            mate = t // 2
            away = d - mate
            far = z + (2 * side - 1) * away
            block = far * Y_SIZE + y + mate * (1 - 2 * y)

            @pl.when((far >= 0) & (far < Z_SIZE) & ((away > 0) | (side == 0)))
            def _():
                @pl.when(mate == 1)
                def _():
                    for part in (1, 2, 3, 4):
                        plane_wait(block, part)

                multiply(lambda q: cols[block, q], block)

            return carry

        return lax.fori_loop(0, 4, one_block, carry)

    lax.fori_loop(1, Z_SIZE + 1, stage, 0)

    for q in (1, 2, 3):
        for j in range(4):
            fit_copy(q, j).wait_send()

    def drain(far, carry):
        for part in range(5):
            for mate in (0, 1):
                if mate == 1 and part > 0:
                    continue
                block = far * Y_SIZE + (y if mate == 0 else 1 - y)
                pl.when(has_up & (far <= z))(lambda: plane_copy(0, block, part).wait_send())
                pl.when(has_down & (far >= z))(lambda: plane_copy(1, block, part).wait_send())
                if part > 0:
                    plane_copy(2, block, part).wait_send()
        return carry

    lax.fori_loop(0, Z_SIZE, drain, 0)
    plane_copy(2, r, 0).wait_send()


def per_device(factors):
    row_count, local_funcs, occupied = factors.shape
    groups = lax.axis_size("fit")
    blocks = lax.axis_size("row")
    if (groups, blocks) != (4, Y_SIZE * Z_SIZE):
        return gathered_by_collectives(factors)
    sub = row_count // groups
    width = local_funcs * occupied
    out_shape = jax.ShapeDtypeStruct((row_count, blocks * sub), jnp.float32)
    out = pl.pallas_call(
        functools.partial(kernel, (local_funcs - 1) * occupied),
        out_shape=out_shape,
        in_specs=[pl.BlockSpec(memory_space=pltpu.VMEM)],
        out_specs=pl.BlockSpec(memory_space=pltpu.VMEM),
        scratch_shapes=[
            pltpu.VMEM((groups - 1, row_count, width), factors.dtype),
            pltpu.VMEM((blocks, groups, sub, width), factors.dtype),
            pltpu.SemaphoreType.DMA((3, 4)),
            pltpu.SemaphoreType.DMA((3, 4)),
            pltpu.SemaphoreType.DMA((3, blocks, 5)),
            pltpu.SemaphoreType.DMA((blocks, 5)),
        ],
        compiler_params=pltpu.CompilerParams(
            collective_id=0, has_side_effects=True, vmem_limit_bytes=58 * 2**20
        ),
        cost_estimate=pl.CostEstimate(
            flops=2 * row_count * blocks * sub * groups * width,
            bytes_accessed=4 * row_count * blocks * sub,
            transcendentals=0,
        ),
    )(factors.reshape(row_count, width))
    return out.reshape(1, row_count, blocks * sub)


def solution(mesh):
    return jax.shard_map(
        per_device,
        mesh=mesh,
        in_specs=(P("row", "fit", None),),
        out_specs=P("fit", "row", None),
        check_vma=False,
    )
```

```python
import jax
import jax.numpy as jnp
from jax import lax
from jax.experimental import pallas as pl
from jax.experimental.pallas import tpu as pltpu
from jax.sharding import PartitionSpec as P

MESH = pl.DeviceIdType.MESH
Z_SIZE = 4
Y_SIZE = 2


def gathered_by_collectives(factors):
    row_count, local_funcs, occupied = factors.shape
    groups = lax.axis_size("fit")
    blocks = lax.axis_size("row")
    sub_width = row_count // groups
    pieces = factors.reshape(groups, sub_width, local_funcs * occupied)
    mine = lax.all_to_all(pieces, "fit", split_axis=0, concat_axis=0)
    columns = lax.all_gather(mine, "row", axis=0)
    rows = lax.all_gather(factors.reshape(row_count, local_funcs * occupied), "fit", axis=0)
    out = lax.dot_general(
        rows, columns, (((0, 2), (1, 3)), ((), ())), preferred_element_type=jnp.float32
    )
    return out.reshape(1, row_count, blocks * sub_width)


def kernel(a_ref, out_ref, acc, rows, near, cols, tiles, fit_send, fit_recv, near_send, near_recv,
           send_sem, recv_sem, tile_send, tile_recv, out_sem):
    f = lax.axis_index("fit")
    r = lax.axis_index("row")
    z = r // Y_SIZE
    y = r % Y_SIZE
    core_mate = f + 1 - 2 * (f % 2)
    x_peer = (f + 2) % 4
    diagonal = (core_mate + 2) % 4
    subs = (f, core_mate, x_peer, diagonal)
    row_count, width = a_ref.shape
    sub = row_count // 4
    half = z // 2
    end_z, inner_z = 3 * half, 1 + half
    far_inner_z, far_end_z = 2 - half, 3 - 3 * half
    is_end = z == end_z
    is_inner = z == inner_z

    def node(at_z, line):
        return at_z * Y_SIZE + line

    end0, end1 = node(end_z, y), node(end_z, 1 - y)
    inner0, inner1 = node(inner_z, y), node(inner_z, 1 - y)
    far_inner0, far_inner1 = node(far_inner_z, y), node(far_inner_z, 1 - y)
    far_end0, far_end1 = node(far_end_z, y), node(far_end_z, 1 - y)
    y_mate = node(z, 1 - y)
    partner = node(end_z + inner_z - z, y)
    PARTNER, FAR, MATE = 0, 1, 2
    targets = (partner, far_inner0, y_mate)
    quarters = range(4)

    def row_slice(s):
        return pl.ds(pl.multiple_of(s * sub, sub), sub)

    def col_slice(block):
        return pl.ds(pl.multiple_of(block * sub, sub), sub)

    def greet(fit, row):
        pl.semaphore_signal(
            pltpu.get_barrier_semaphore(), inc=1, device_id=(fit, row), device_id_type=MESH
        )

    greet(core_mate, r)
    greet(x_peer, r)
    greet(f, y_mate)
    greet(f, partner)
    pl.when(is_inner)(lambda: greet(f, far_inner0))
    pl.semaphore_wait(pltpu.get_barrier_semaphore(), 4 + is_inner.astype(jnp.int32))

    def fit_copy(q, j):
        if q == 2:
            target, s = x_peer, subs[2 ^ j]
        else:
            target, s = core_mate, subs[1 ^ j]
        source = rows.at[1, row_slice(s)] if q == 3 else a_ref.at[row_slice(s)]
        return pltpu.make_async_remote_copy(
            src_ref=source,
            dst_ref=rows.at[q - 1, row_slice(s)],
            send_sem=fit_send.at[q - 1, j],
            recv_sem=fit_recv.at[q - 1, j],
            device_id=(target, r),
            device_id_type=MESH,
        )

    def fit_wait(q, j):
        landed = rows.at[q - 1, row_slice(subs[j])]
        pltpu.make_async_remote_copy(
            src_ref=landed,
            dst_ref=landed,
            send_sem=fit_send.at[q - 1, j],
            recv_sem=fit_recv.at[q - 1, j],
            device_id=(core_mate, r),
            device_id_type=MESH,
        ).wait_recv()

    def near_copy(j, q):
        if j == 3:
            source, target = near.at[1, q ^ 1], core_mate
        else:
            source, target = cols.at[end0, q ^ j], (core_mate if j == 1 else x_peer)
        return pltpu.make_async_remote_copy(
            src_ref=source,
            dst_ref=near.at[j - 1, q],
            send_sem=near_send.at[j - 1, q],
            recv_sem=near_recv.at[j - 1, q],
            device_id=(target, r),
            device_id_type=MESH,
        )

    def plane_copy(direction, block, q, source=None):
        slot = cols.at[block, q]
        return pltpu.make_async_remote_copy(
            src_ref=slot if source is None else source,
            dst_ref=slot,
            send_sem=send_sem.at[direction, block, q],
            recv_sem=recv_sem.at[block, q],
            device_id=(f, targets[direction]),
            device_id_type=MESH,
        )

    def plane_wait(block, q):
        plane_copy(MATE, block, q).wait_recv()

    def pass_on(block, q, *directions):
        plane_wait(block, q)
        for direction in directions:
            plane_copy(direction, block, q).start()

    def send_own(q):
        source = (a_ref if q == 0 else rows.at[q - 1]).at[row_slice(f)]
        pl.when(is_inner)(lambda: plane_copy(FAR, r, q, source).start())
        plane_copy(PARTNER, r, q, source).start()
        plane_copy(MATE, r, q, source).start()

    def tile_copy(block, k, j):
        return pltpu.make_async_remote_copy(
            src_ref=tiles.at[k, j],
            dst_ref=acc.at[row_slice(subs[j]), col_slice(block)],
            send_sem=tile_send.at[k, j],
            recv_sem=tile_recv.at[k, j],
            device_id=(f, partner),
            device_id_type=MESH,
        )

    def out_copy(block):
        return pltpu.make_async_copy(
            acc.at[:, col_slice(block)], out_ref.at[:, col_slice(block)], out_sem.at[block]
        )

    dims = (((1,), (1,)), ((), ()))

    def dot(left, right):
        return lax.dot_general(left, right, dims, preferred_element_type=jnp.float32)

    def multiply(operand, block):
        tile = min(512, row_count)

        @pl.loop(0, row_count // tile)
        def _(i):
            here = pl.ds(pl.multiple_of(i * tile, tile), tile)
            total = dot(a_ref[here, :], operand(0))
            for q in (1, 2, 3):
                total += dot(rows[q - 1, here, :], operand(q))
            acc[here, col_slice(block)] = total

        out_copy(block).start()

    def multiply_block(block):
        multiply(lambda q: cols[block, q], block)

    def near_tile(block, k, j):
        total = dot(cols[end0, 0] if j == 0 else near[j - 1, 0], cols[block, 0])
        for q in (1, 2, 3):
            total += dot(cols[end0, q] if j == 0 else near[j - 1, q], cols[block, q])
        tiles[k, j] = total
        tile_copy(block, k, j).start()

    def finish_fit():
        for j in (2, 3):
            fit_wait(2, j)
            fit_copy(3, j ^ 1).start()
        for j in (1, 2, 3):
            fit_wait(1, j)
            fit_wait(3, j)
        multiply(
            lambda q: a_ref[row_slice(f), :] if q == 0 else rows[q - 1, row_slice(f), :], r
        )

    fit_copy(2, 0).start()
    fit_copy(1, 0).start()
    send_own(0)
    fit_copy(2, 1).start()
    for j in (1, 2, 3):
        fit_copy(1, j).start()
    fit_wait(1, 0)
    send_own(1)

    @pl.when(is_inner)
    def _():
        pass_on(inner1, 0, FAR)
        pass_on(end0, 0, FAR)
        near_copy(1, 1).start()

    fit_wait(2, 0)
    send_own(2)
    fit_copy(2, 2).start()
    fit_wait(2, 1)
    fit_copy(3, 0).start()
    fit_copy(2, 3).start()
    fit_copy(3, 1).start()
    fit_wait(3, 0)
    send_own(3)

    @pl.when(is_inner)
    def _():
        near_copy(2, 2).start()
        plane_wait(far_inner0, 0)
        for q in (1, 2, 3):
            pass_on(end0, q, FAR)
            near_copy(1, q ^ 1).start()
            near_copy(2, q ^ 2).start()
            pass_on(far_inner0, q, MATE)
        finish_fit()
        pass_on(end1, 0, FAR)
        for q in (1, 2, 3):
            plane_wait(inner1, q)
        multiply_block(inner1)
        multiply_block(end0)
        multiply_block(far_inner0)
        near_copy(2, 2).wait_recv()
        near_copy(3, 3).start()
        plane_wait(far_end0, 0)
        for q in quarters:
            near_copy(1, q).wait_recv()
        for j in (0, 1):
            near_tile(far_inner0, 0, j)
        pass_on(far_end0, 1, MATE)
        plane_wait(far_inner1, 0)
        for q in (1, 2, 3):
            plane_wait(far_inner1, q)
        for j in (0, 1):
            near_tile(far_inner1, 1, j)
        multiply_block(far_inner1)
        for q in (3, 0, 1):
            near_copy(2, q).wait_recv()
            near_copy(3, q ^ 1).start()
        for q in (2, 3):
            pass_on(far_end0, q, MATE)
        for j in (0, 1):
            near_tile(far_end0, 2, j)
        for q in quarters:
            near_copy(3, q).wait_recv()
        for j in (2, 3):
            near_tile(far_inner0, 0, j)
            near_tile(far_inner1, 1, j)
            near_tile(far_end0, 2, j)
        multiply_block(far_end0)
        for q in (1, 2, 3):
            plane_wait(end1, q)
        multiply_block(end1)
        for q in quarters:
            plane_wait(far_end1, q)
        for j in quarters:
            near_tile(far_end1, 3, j)
        multiply_block(far_end1)

    @pl.when(is_end)
    def _():
        for q in quarters:
            pass_on(end1, q, PARTNER)
            pass_on(inner0, q, MATE)
        finish_fit()
        multiply_block(end1)
        multiply_block(inner0)
        for q in quarters:
            plane_wait(inner1, q)
        multiply_block(inner1)
        for k, block in enumerate((far_inner0, far_inner1, far_end0, far_end1)):
            for j in quarters:
                tile_copy(block, k, j).wait_recv()
            out_copy(block).start()

    for q in quarters:
        plane_copy(PARTNER, r, q).wait_send()
        plane_copy(MATE, r, q).wait_send()
        for j in (1, 2, 3):
            fit_copy(j, q).wait_send()

    @pl.when(is_inner)
    def _():
        for q in quarters:
            plane_copy(FAR, r, q).wait_send()
            plane_copy(FAR, end0, q).wait_send()
            for j in (1, 2, 3):
                near_copy(j, q).wait_send()
            if q > 0:
                plane_copy(MATE, far_inner0, q).wait_send()
                plane_copy(MATE, far_end0, q).wait_send()
        plane_copy(FAR, inner1, 0).wait_send()
        plane_copy(FAR, end1, 0).wait_send()
        for k, block in enumerate((far_inner0, far_inner1, far_end0, far_end1)):
            for j in quarters:
                tile_copy(block, k, j).wait_send()

    @pl.when(is_end)
    def _():
        for q in quarters:
            plane_copy(PARTNER, end1, q).wait_send()
            plane_copy(MATE, inner0, q).wait_send()

    for block in range(Y_SIZE * Z_SIZE):
        out_copy(block).wait()


def per_device(factors):
    row_count, local_funcs, occupied = factors.shape
    groups = lax.axis_size("fit")
    blocks = lax.axis_size("row")
    if (groups, blocks) != (4, Y_SIZE * Z_SIZE):
        return gathered_by_collectives(factors)
    sub = row_count // groups
    width = local_funcs * occupied
    out_shape = jax.ShapeDtypeStruct((row_count, blocks * sub), jnp.float32)
    out = pl.pallas_call(
        kernel,
        out_shape=out_shape,
        in_specs=[pl.BlockSpec(memory_space=pltpu.VMEM)],
        out_specs=pl.BlockSpec(memory_space=pl.ANY),
        scratch_shapes=[
            pltpu.VMEM((row_count, blocks * sub), jnp.float32),
            pltpu.VMEM((groups - 1, row_count, width), factors.dtype),
            pltpu.VMEM((groups - 1, groups, sub, width), factors.dtype),
            pltpu.VMEM((blocks, groups, sub, width), factors.dtype),
            pltpu.VMEM((groups, groups, sub, sub), jnp.float32),
            pltpu.SemaphoreType.DMA((3, 4)),
            pltpu.SemaphoreType.DMA((3, 4)),
            pltpu.SemaphoreType.DMA((3, 4)),
            pltpu.SemaphoreType.DMA((3, 4)),
            pltpu.SemaphoreType.DMA((3, blocks, 4)),
            pltpu.SemaphoreType.DMA((blocks, 4)),
            pltpu.SemaphoreType.DMA((4, 4)),
            pltpu.SemaphoreType.DMA((4, 4)),
            pltpu.SemaphoreType.DMA((blocks,)),
        ],
        compiler_params=pltpu.CompilerParams(
            collective_id=0, has_side_effects=True, vmem_limit_bytes=62 * 2**20
        ),
        cost_estimate=pl.CostEstimate(
            flops=2 * row_count * blocks * sub * groups * width,
            bytes_accessed=4 * row_count * blocks * sub,
            transcendentals=0,
        ),
    )(factors.reshape(row_count, width))
    return out.reshape(1, row_count, blocks * sub)


def solution(mesh):
    return jax.shard_map(
        per_device,
        mesh=mesh,
        in_specs=(P("row", "fit", None),),
        out_specs=P("fit", "row", None),
        check_vma=False,
    )
```

```python
import jax
import jax.numpy as jnp
from jax import lax
from jax.experimental import pallas as pl
from jax.experimental.pallas import tpu as pltpu
from jax.sharding import PartitionSpec as P

MESH = pl.DeviceIdType.MESH
Z_SIZE = 4
Y_SIZE = 2


def gathered_by_collectives(factors):
    row_count, local_funcs, occupied = factors.shape
    groups = lax.axis_size("fit")
    blocks = lax.axis_size("row")
    sub_width = row_count // groups
    pieces = factors.reshape(groups, sub_width, local_funcs * occupied)
    mine = lax.all_to_all(pieces, "fit", split_axis=0, concat_axis=0)
    columns = lax.all_gather(mine, "row", axis=0)
    rows = lax.all_gather(factors.reshape(row_count, local_funcs * occupied), "fit", axis=0)
    out = lax.dot_general(
        rows, columns, (((0, 2), (1, 3)), ((), ())), preferred_element_type=jnp.float32
    )
    return out.reshape(1, row_count, blocks * sub_width)


def kernel(a_hbm, out_ref, a_ref, acc, rows, near, cols, tiles, fit_send, fit_recv, near_send, near_recv,
           send_sem, recv_sem, tile_send, tile_recv, out_sem, load_sem):
    f = lax.axis_index("fit")
    r = lax.axis_index("row")
    z = r // Y_SIZE
    y = r % Y_SIZE
    core_mate = f + 1 - 2 * (f % 2)
    x_peer = (f + 2) % 4
    diagonal = (core_mate + 2) % 4
    subs = (f, core_mate, x_peer, diagonal)
    row_count, width = a_hbm.shape
    sub = row_count // 4
    half = z // 2
    end_z, inner_z = 3 * half, 1 + half
    far_inner_z, far_end_z = 2 - half, 3 - 3 * half
    is_end = z == end_z
    is_inner = z == inner_z

    def node(at_z, line):
        return at_z * Y_SIZE + line

    end0, end1 = node(end_z, y), node(end_z, 1 - y)
    inner0, inner1 = node(inner_z, y), node(inner_z, 1 - y)
    far_inner0, far_inner1 = node(far_inner_z, y), node(far_inner_z, 1 - y)
    far_end0, far_end1 = node(far_end_z, y), node(far_end_z, 1 - y)
    y_mate = node(z, 1 - y)
    partner = node(end_z + inner_z - z, y)
    PARTNER, FAR, MATE = 0, 1, 2
    targets = (partner, far_inner0, y_mate)
    quarters = range(4)

    def row_slice(s):
        return pl.ds(pl.multiple_of(s * sub, sub), sub)

    def col_slice(block):
        return pl.ds(pl.multiple_of(block * sub, sub), sub)

    def greet(fit, row):
        pl.semaphore_signal(
            pltpu.get_barrier_semaphore(), inc=1, device_id=(fit, row), device_id_type=MESH
        )

    greet(core_mate, r)
    greet(x_peer, r)
    greet(f, y_mate)
    greet(f, partner)
    pl.when(is_inner)(lambda: greet(f, far_inner0))
    pl.semaphore_wait(pltpu.get_barrier_semaphore(), 4 + is_inner.astype(jnp.int32))

    def fit_copy(q, j):
        if q == 2:
            target, s = x_peer, subs[2 ^ j]
        else:
            target, s = core_mate, subs[1 ^ j]
        source = rows.at[1, row_slice(s)] if q == 3 else a_hbm.at[row_slice(s)]
        return pltpu.make_async_remote_copy(
            src_ref=source,
            dst_ref=rows.at[q - 1, row_slice(s)],
            send_sem=fit_send.at[q - 1, j],
            recv_sem=fit_recv.at[q - 1, j],
            device_id=(target, r),
            device_id_type=MESH,
        )

    def fit_wait(q, j):
        landed = rows.at[q - 1, row_slice(subs[j])]
        pltpu.make_async_remote_copy(
            src_ref=landed,
            dst_ref=landed,
            send_sem=fit_send.at[q - 1, j],
            recv_sem=fit_recv.at[q - 1, j],
            device_id=(core_mate, r),
            device_id_type=MESH,
        ).wait_recv()

    def near_copy(j, q):
        if j == 3:
            source, target = near.at[1, q ^ 1], core_mate
        else:
            source, target = cols.at[end0, q ^ j], (core_mate if j == 1 else x_peer)
        return pltpu.make_async_remote_copy(
            src_ref=source,
            dst_ref=near.at[j - 1, q],
            send_sem=near_send.at[j - 1, q],
            recv_sem=near_recv.at[j - 1, q],
            device_id=(target, r),
            device_id_type=MESH,
        )

    def plane_copy(direction, block, q, source=None):
        slot = cols.at[block, q]
        return pltpu.make_async_remote_copy(
            src_ref=slot if source is None else source,
            dst_ref=slot,
            send_sem=send_sem.at[direction, block, q],
            recv_sem=recv_sem.at[block, q],
            device_id=(f, targets[direction]),
            device_id_type=MESH,
        )

    def plane_wait(block, q):
        plane_copy(MATE, block, q).wait_recv()

    def pass_on(block, q, *directions):
        plane_wait(block, q)
        for direction in directions:
            plane_copy(direction, block, q).start()

    def send_own(q):
        source = (a_hbm if q == 0 else rows.at[q - 1]).at[row_slice(f)]
        pl.when(is_inner)(lambda: plane_copy(FAR, r, q, source).start())
        plane_copy(PARTNER, r, q, source).start()
        pl.when(is_end | (q == 0))(lambda: plane_copy(MATE, r, q, source).start())

    def tile_copy(block, k, j):
        return pltpu.make_async_remote_copy(
            src_ref=tiles.at[k, j],
            dst_ref=acc.at[row_slice(subs[j]), col_slice(block)],
            send_sem=tile_send.at[k, j],
            recv_sem=tile_recv.at[k, j],
            device_id=(f, partner),
            device_id_type=MESH,
        )

    def out_copy(block):
        return pltpu.make_async_copy(
            acc.at[:, col_slice(block)], out_ref.at[:, col_slice(block)], out_sem.at[block]
        )

    dims = (((1,), (1,)), ((), ()))

    def dot(left, right):
        return lax.dot_general(left, right, dims, preferred_element_type=jnp.float32)

    def multiply(operand, block):
        tile = min(512, row_count)

        @pl.loop(0, row_count // tile)
        def _(i):
            here = pl.ds(pl.multiple_of(i * tile, tile), tile)
            total = dot(a_ref[here, :], operand(0))
            for q in (1, 2, 3):
                total += dot(rows[q - 1, here, :], operand(q))
            acc[here, col_slice(block)] = total

        out_copy(block).start()

    def multiply_block(block):
        multiply(lambda q: cols[block, q], block)

    def near_tile(block, k, j):
        total = dot(cols[end0, 0] if j == 0 else near[j - 1, 0], cols[block, 0])
        for q in (1, 2, 3):
            total += dot(cols[end0, q] if j == 0 else near[j - 1, q], cols[block, q])
        tiles[k, j] = total
        tile_copy(block, k, j).start()

    load = pltpu.make_async_copy(a_hbm, a_ref, load_sem)

    def spread_x_peer(j):
        fit_wait(2, j)
        fit_copy(3, j ^ 1).start()

    def finish_fit():
        for j in (1, 2, 3):
            fit_wait(1, j)
            fit_wait(3, j)
        load.wait()
        multiply(
            lambda q: a_ref[row_slice(f), :] if q == 0 else rows[q - 1, row_slice(f), :], r
        )

    fit_copy(2, 0).start()
    fit_copy(1, 0).start()
    send_own(0)
    fit_copy(2, 1).start()
    for j in (1, 2, 3):
        fit_copy(1, j).start()
    load.start()
    fit_wait(1, 0)
    send_own(1)

    @pl.when(is_inner)
    def _():
        plane_wait(end0, 0)
        near_copy(1, 1).start()

    fit_wait(2, 0)
    send_own(2)
    pl.when(is_end)(lambda: fit_copy(2, 2).start())
    pl.when(is_inner)(lambda: near_copy(2, 2).start())
    fit_wait(2, 1)
    fit_copy(3, 0).start()
    pl.when(is_end)(lambda: fit_copy(2, 3).start())
    fit_copy(3, 1).start()
    fit_wait(3, 0)
    send_own(3)

    @pl.when(is_inner)
    def _():
        pass_on(far_inner0, 0, MATE)
        for q in (1, 2, 3):
            pass_on(far_inner0, q, MATE)
            pass_on(end0, q, FAR)
            near_copy(1, q ^ 1).start()
            near_copy(2, q ^ 2).start()
        plane_copy(FAR, end0, 0).start()
        fit_copy(2, 2).start()
        fit_copy(2, 3).start()
        for q in (2, 3):
            near_copy(2, q).wait_recv()
            near_copy(3, q ^ 1).start()
        pass_on(end1, 0, FAR)
        pass_on(far_end0, 1, MATE)
        near_copy(2, 0).wait_recv()
        near_copy(3, 1).start()
        for q in quarters:
            near_copy(1, q).wait_recv()
            plane_wait(far_inner1, q)
        for j in (0, 1):
            near_tile(far_inner0, 0, j)
            near_tile(far_inner1, 1, j)
        near_copy(2, 1).wait_recv()
        near_copy(3, 0).start()
        pass_on(far_end0, 2, MATE)
        for q in quarters:
            near_copy(3, q).wait_recv()
        for j in (2, 3):
            near_tile(far_inner0, 0, j)
            near_tile(far_inner1, 1, j)
        pass_on(far_end0, 3, MATE)
        plane_copy(MATE, r, 1, rows.at[0, row_slice(f)]).start()
        spread_x_peer(2)
        plane_wait(far_end0, 0)
        for j in quarters:
            near_tile(far_end0, 2, j)
        spread_x_peer(3)
        finish_fit()
        multiply_block(end0)
        multiply_block(far_inner0)
        multiply_block(far_inner1)
        for q in quarters:
            plane_wait(far_end1, q)
        for j in quarters:
            near_tile(far_end1, 3, j)
        multiply_block(far_end0)
        multiply_block(far_end1)
        for q in (1, 2, 3):
            plane_wait(end1, q)
        multiply_block(end1)
        for q in quarters:
            plane_wait(inner1, q)
        multiply_block(inner1)

    @pl.when(is_end)
    def _():
        for q in quarters:
            pass_on(end1, q, PARTNER)
            pass_on(inner0, q, MATE)
        spread_x_peer(2)
        spread_x_peer(3)
        finish_fit()
        multiply_block(end1)
        multiply_block(inner0)
        plane_wait(inner1, 0)
        plane_wait(inner1, 1)
        pass_on(inner1, 2, PARTNER)
        pass_on(inner1, 3, PARTNER)
        multiply_block(inner1)
        for k, block in enumerate((far_inner0, far_inner1, far_end0, far_end1)):
            for j in quarters:
                tile_copy(block, k, j).wait_recv()
            out_copy(block).start()

    for q in quarters:
        plane_copy(PARTNER, r, q).wait_send()
        for j in (1, 2, 3):
            fit_copy(j, q).wait_send()
    for q in (0, 1):
        plane_copy(MATE, r, q).wait_send()

    @pl.when(is_inner)
    def _():
        for q in quarters:
            plane_copy(FAR, r, q).wait_send()
            plane_copy(FAR, end0, q).wait_send()
            plane_copy(MATE, far_inner0, q).wait_send()
            for j in (1, 2, 3):
                near_copy(j, q).wait_send()
            if q > 0:
                plane_copy(MATE, far_end0, q).wait_send()
        plane_copy(FAR, end1, 0).wait_send()
        for k, block in enumerate((far_inner0, far_inner1, far_end0, far_end1)):
            for j in quarters:
                tile_copy(block, k, j).wait_send()

    @pl.when(is_end)
    def _():
        for q in quarters:
            plane_copy(PARTNER, end1, q).wait_send()
            plane_copy(MATE, inner0, q).wait_send()
            if q > 1:
                plane_copy(MATE, r, q).wait_send()
                plane_copy(PARTNER, inner1, q).wait_send()

    for block in range(Y_SIZE * Z_SIZE):
        out_copy(block).wait()


def per_device(factors):
    row_count, local_funcs, occupied = factors.shape
    groups = lax.axis_size("fit")
    blocks = lax.axis_size("row")
    if (groups, blocks) != (4, Y_SIZE * Z_SIZE):
        return gathered_by_collectives(factors)
    sub = row_count // groups
    width = local_funcs * occupied
    out_shape = jax.ShapeDtypeStruct((row_count, blocks * sub), jnp.float32)
    out = pl.pallas_call(
        kernel,
        out_shape=out_shape,
        in_specs=[pl.BlockSpec(memory_space=pl.ANY)],
        out_specs=pl.BlockSpec(memory_space=pl.ANY),
        scratch_shapes=[
            pltpu.VMEM((row_count, width), factors.dtype),
            pltpu.VMEM((row_count, blocks * sub), jnp.float32),
            pltpu.VMEM((groups - 1, row_count, width), factors.dtype),
            pltpu.VMEM((groups - 1, groups, sub, width), factors.dtype),
            pltpu.VMEM((blocks, groups, sub, width), factors.dtype),
            pltpu.VMEM((groups, groups, sub, sub), jnp.float32),
            pltpu.SemaphoreType.DMA((3, 4)),
            pltpu.SemaphoreType.DMA((3, 4)),
            pltpu.SemaphoreType.DMA((3, 4)),
            pltpu.SemaphoreType.DMA((3, 4)),
            pltpu.SemaphoreType.DMA((3, blocks, 4)),
            pltpu.SemaphoreType.DMA((blocks, 4)),
            pltpu.SemaphoreType.DMA((4, 4)),
            pltpu.SemaphoreType.DMA((4, 4)),
            pltpu.SemaphoreType.DMA((blocks,)),
            pltpu.SemaphoreType.DMA,
        ],
        compiler_params=pltpu.CompilerParams(
            collective_id=0, has_side_effects=True, vmem_limit_bytes=62 * 2**20
        ),
        cost_estimate=pl.CostEstimate(
            flops=2 * row_count * blocks * sub * groups * width,
            bytes_accessed=4 * row_count * blocks * sub,
            transcendentals=0,
        ),
    )(factors.reshape(row_count, width))
    return out.reshape(1, row_count, blocks * sub)


def solution(mesh):
    return jax.shard_map(
        per_device,
        mesh=mesh,
        in_specs=(P("row", "fit", None),),
        out_specs=P("fit", "row", None),
        check_vma=False,
    )
```

```python
import jax
import jax.numpy as jnp
from jax import lax
from jax.experimental import pallas as pl
from jax.experimental.pallas import tpu as pltpu
from jax.sharding import PartitionSpec as P

MESH = pl.DeviceIdType.MESH
Z_SIZE = 4
Y_SIZE = 2


def gathered_by_collectives(factors):
    row_count, local_funcs, occupied = factors.shape
    groups = lax.axis_size("fit")
    blocks = lax.axis_size("row")
    sub_width = row_count // groups
    pieces = factors.reshape(groups, sub_width, local_funcs * occupied)
    mine = lax.all_to_all(pieces, "fit", split_axis=0, concat_axis=0)
    columns = lax.all_gather(mine, "row", axis=0)
    rows = lax.all_gather(factors.reshape(row_count, local_funcs * occupied), "fit", axis=0)
    out = lax.dot_general(
        rows, columns, (((0, 2), (1, 3)), ((), ())), preferred_element_type=jnp.float32
    )
    return out.reshape(1, row_count, blocks * sub_width)


def kernel(a_hbm, out_ref, a_ref, acc, rows, near, cols, tiles, fit_send, fit_recv, near_send, near_recv,
           send_sem, recv_sem, tile_send, tile_recv, out_sem, load_sem):
    f = lax.axis_index("fit")
    r = lax.axis_index("row")
    z = r // Y_SIZE
    y = r % Y_SIZE
    core_mate = f + 1 - 2 * (f % 2)
    x_peer = (f + 2) % 4
    diagonal = (core_mate + 2) % 4
    subs = (f, core_mate, x_peer, diagonal)
    row_count, width = a_hbm.shape
    sub = row_count // 4
    narrow = sub // 2
    half = z // 2
    end_z, inner_z = 3 * half, 1 + half
    far_inner_z, far_end_z = 2 - half, 3 - 3 * half
    is_end = z == end_z
    is_inner = z == inner_z

    def node(at_z, line):
        return at_z * Y_SIZE + line

    end0, end1 = node(end_z, y), node(end_z, 1 - y)
    inner0, inner1 = node(inner_z, y), node(inner_z, 1 - y)
    far_inner0, far_inner1 = node(far_inner_z, y), node(far_inner_z, 1 - y)
    far_end0, far_end1 = node(far_end_z, y), node(far_end_z, 1 - y)
    y_mate = node(z, 1 - y)
    partner = node(end_z + inner_z - z, y)
    PARTNER, FAR, MATE = 0, 1, 2
    targets = (partner, far_inner0, y_mate)
    quarters = range(4)

    def row_slice(s):
        return pl.ds(pl.multiple_of(s * sub, sub), sub)

    def col_slice(block):
        return pl.ds(pl.multiple_of(block * sub, sub), sub)

    def greet(fit, row):
        pl.semaphore_signal(
            pltpu.get_barrier_semaphore(), inc=1, device_id=(fit, row), device_id_type=MESH
        )

    greet(core_mate, r)
    greet(x_peer, r)
    greet(f, y_mate)
    greet(f, partner)
    pl.when(is_inner)(lambda: greet(f, far_inner0))
    pl.semaphore_wait(pltpu.get_barrier_semaphore(), 4 + is_inner.astype(jnp.int32))

    def fit_copy(q, j):
        if q == 2:
            target, s = x_peer, subs[2 ^ j]
        else:
            target, s = core_mate, subs[1 ^ j]
        source = rows.at[1, row_slice(s)] if q == 3 else a_hbm.at[row_slice(s)]
        return pltpu.make_async_remote_copy(
            src_ref=source,
            dst_ref=rows.at[q - 1, row_slice(s)],
            send_sem=fit_send.at[q - 1, j],
            recv_sem=fit_recv.at[q - 1, j],
            device_id=(target, r),
            device_id_type=MESH,
        )

    def fit_wait(q, j):
        landed = rows.at[q - 1, row_slice(subs[j])]
        pltpu.make_async_remote_copy(
            src_ref=landed,
            dst_ref=landed,
            send_sem=fit_send.at[q - 1, j],
            recv_sem=fit_recv.at[q - 1, j],
            device_id=(core_mate, r),
            device_id_type=MESH,
        ).wait_recv()

    def near_copy(j, q):
        if j == 3:
            source, target = near.at[1, q ^ 1], core_mate
        else:
            source, target = cols.at[end0, q ^ j], (core_mate if j == 1 else x_peer)
        return pltpu.make_async_remote_copy(
            src_ref=source,
            dst_ref=near.at[j - 1, q],
            send_sem=near_send.at[j - 1, q],
            recv_sem=near_recv.at[j - 1, q],
            device_id=(target, r),
            device_id_type=MESH,
        )

    def plane_copy(direction, block, q, h, source=None):
        slot = cols.at[block, q, pl.ds(h * narrow, narrow)]
        return pltpu.make_async_remote_copy(
            src_ref=slot if source is None else source,
            dst_ref=slot,
            send_sem=send_sem.at[direction, block, 2 * q + h],
            recv_sem=recv_sem.at[block, 2 * q + h],
            device_id=(f, targets[direction]),
            device_id_type=MESH,
        )

    def part_sent(direction, block, q):
        for h in (0, 1):
            plane_copy(direction, block, q, h).wait_send()

    def plane_wait(block, q, halves=(0, 1)):
        for h in halves:
            plane_copy(MATE, block, q, h).wait_recv()

    def pass_on(block, q, direction, halves=(0, 1)):
        for h in halves:
            plane_wait(block, q, (h,))
            plane_copy(direction, block, q, h).start()

    def send_own_half(direction, q, h):
        here = pl.ds(pl.multiple_of(f * sub + h * narrow, narrow), narrow)
        source = (a_hbm if q == 0 else rows.at[q - 1]).at[here]
        plane_copy(direction, r, q, h, source).start()

    def send_own(q):
        for h in (0, 1):
            pl.when(is_inner)(lambda: send_own_half(FAR, q, h))
            send_own_half(PARTNER, q, h)
            pl.when(is_end | (q == 0))(lambda: send_own_half(MATE, q, h))

    def tile_copy(block, k, j, h, size):
        return pltpu.make_async_remote_copy(
            src_ref=tiles.at[k, j, :, pl.ds(h * narrow, size)],
            dst_ref=acc.at[
                row_slice(subs[j]),
                pl.ds(pl.multiple_of(block * sub + h * narrow, narrow), size),
            ],
            send_sem=tile_send.at[k, 2 * j + h],
            recv_sem=tile_recv.at[k, 2 * j + h],
            device_id=(f, partner),
            device_id_type=MESH,
        )

    def tile_copies():
        far = (far_inner0, far_inner1, far_end0, far_end1)
        return [
            [
                tile_copy(block, k, j, h, sub if k < 2 else narrow)
                for j in quarters
                for h in ((0,) if k < 2 else (0, 1))
            ]
            for k, block in enumerate(far)
        ]

    def out_copy(block):
        return pltpu.make_async_copy(
            acc.at[:, col_slice(block)], out_ref.at[:, col_slice(block)], out_sem.at[block]
        )

    dims = (((1,), (1,)), ((), ()))

    def dot(left, right):
        return lax.dot_general(left, right, dims, preferred_element_type=jnp.float32)

    def multiply(operand, block):
        tile = min(512, row_count)

        @pl.loop(0, row_count // tile)
        def _(i):
            here = pl.ds(pl.multiple_of(i * tile, tile), tile)
            total = dot(a_ref[here, :], operand(0))
            for q in (1, 2, 3):
                total += dot(rows[q - 1, here, :], operand(q))
            acc[here, col_slice(block)] = total

        out_copy(block).start()

    def multiply_block(block):
        multiply(lambda q: cols[block, q], block)

    def multiply_rows(operand, block, early):
        part = f // 2 if early else 1 - f // 2
        here = pl.ds(pl.multiple_of(part * (2 * sub), 2 * sub), 2 * sub)
        total = dot(a_ref[here, :], operand(0))
        for q in (1, 2, 3):
            total += dot(rows[q - 1, here, :], operand(q))
        acc[here, col_slice(block)] = total
        if not early:
            out_copy(block).start()

    def multiply_blocks(first, count, early):
        @pl.loop(0, count)
        def _(i):
            block = first + i
            multiply_rows(lambda q: cols[block, q], block, early)

    def own_operand(q):
        return a_ref[row_slice(f), :] if q == 0 else rows[q - 1, row_slice(f), :]

    def near_tile(block, k, j, h, size):
        here = pl.ds(h * narrow, size)
        total = dot(cols[end0, 0] if j == 0 else near[j - 1, 0], cols[block, 0, here])
        for q in (1, 2, 3):
            total += dot(cols[end0, q] if j == 0 else near[j - 1, q], cols[block, q, here])
        tiles[k, j, :, here] = total
        tile_copy(block, k, j, h, size).start()

    load = pltpu.make_async_copy(a_hbm, a_ref, load_sem)

    def spread_x_peer(j):
        fit_wait(2, j)
        fit_copy(3, j ^ 1).start()

    fit_copy(2, 0).start()
    fit_copy(1, 0).start()
    send_own(0)
    fit_copy(2, 1).start()
    for j in (1, 2, 3):
        fit_copy(1, j).start()
    load.start()
    fit_wait(1, 0)
    send_own(1)

    @pl.when(is_inner)
    def _():
        plane_wait(end0, 0)
        near_copy(1, 1).start()

    fit_wait(2, 0)
    send_own(2)
    pl.when(is_end)(lambda: fit_copy(2, 2).start())
    pl.when(is_inner)(lambda: near_copy(2, 2).start())
    fit_wait(2, 1)
    fit_copy(3, 0).start()
    pl.when(is_end)(lambda: fit_copy(2, 3).start())
    fit_copy(3, 1).start()
    fit_wait(3, 0)
    send_own(3)

    @pl.when(is_inner)
    def _():
        plane_copy(FAR, end0, 0, 0).start()
        pass_on(far_inner0, 0, MATE)
        for q in (1, 2, 3):
            pass_on(far_inner0, q, MATE)
            plane_wait(end0, q)
            plane_copy(FAR, end0, q, 0).start()
            near_copy(1, q ^ 1).start()
            near_copy(2, q ^ 2).start()
        for q in quarters:
            plane_copy(FAR, end0, q, 1).start()
        fit_copy(2, 2).start()
        fit_copy(2, 3).start()
        for q in quarters:
            near_copy(1, q).wait_recv()
        for j in (0, 1):
            near_tile(far_inner0, 0, j, 0, sub)
        for q in (2, 3):
            near_copy(2, q).wait_recv()
            near_copy(3, q ^ 1).start()
        pass_on(far_end0, 0, MATE, (0,))
        load.wait()
        fit_wait(1, 1)
        fit_wait(3, 1)
        multiply_rows(own_operand, r, True)
        pass_on(far_end0, 1, MATE, (0,))
        near_copy(2, 0).wait_recv()
        near_copy(3, 1).start()
        for q in quarters:
            plane_wait(far_inner1, q)
        for j in (0, 1):
            near_tile(far_inner1, 1, j, 0, sub)
        pass_on(far_end0, 2, MATE, (0,))
        near_copy(2, 1).wait_recv()
        near_copy(3, 0).start()
        pass_on(far_end0, 3, MATE, (0,))
        for q in quarters:
            near_copy(3, q).wait_recv()
        for j in (2, 3):
            near_tile(far_inner0, 0, j, 0, sub)
            near_tile(far_inner1, 1, j, 0, sub)
        for j in quarters:
            near_tile(far_end0, 2, j, 0, narrow)
        pass_on(far_end0, 0, MATE, (1,))
        for q in quarters:
            plane_wait(far_end1, q, (0,))
        for j in quarters:
            near_tile(far_end1, 3, j, 0, narrow)
        pass_on(far_end0, 1, MATE, (1,))
        multiply_rows(lambda q: cols[end0, q], end0, True)
        spread_x_peer(2)
        pass_on(far_end0, 2, MATE, (1,))
        multiply_blocks(node(far_inner_z, 0), 2, True)
        pass_on(far_end0, 3, MATE, (1,))
        for h in (0, 1):
            send_own_half(MATE, 1, h)
        for j in quarters:
            near_tile(far_end0, 2, j, 1, narrow)
        spread_x_peer(3)
        multiply_rows(lambda q: cols[far_end0, q], far_end0, True)
        for q in quarters:
            plane_wait(far_end1, q, (1,))
        for j in quarters:
            near_tile(far_end1, 3, j, 1, narrow)
        multiply_rows(lambda q: cols[far_end1, q], far_end1, True)
        for j in (2, 3):
            fit_wait(1, j)
            fit_wait(3, j)
        multiply_rows(own_operand, r, False)
        multiply_rows(lambda q: cols[end0, q], end0, False)
        multiply_blocks(4 * (1 - half), 4, False)
        for q in quarters:
            plane_wait(end1, q)
        multiply_block(end1)
        for q in quarters:
            plane_wait(inner1, q)
        multiply_block(inner1)

    @pl.when(is_end)
    def _():
        for q in quarters:
            pass_on(end1, q, PARTNER)
            pass_on(inner0, q, MATE)
        spread_x_peer(2)
        spread_x_peer(3)
        load.wait()
        for j in (1, 2, 3):
            fit_wait(1, j)
            fit_wait(3, j)
        multiply(own_operand, r)
        multiply_block(end1)
        multiply_block(inner0)
        plane_wait(inner1, 0)
        plane_wait(inner1, 1)
        pass_on(inner1, 2, PARTNER)
        pass_on(inner1, 3, PARTNER)
        multiply_block(inner1)
        far = (far_inner0, far_inner1, far_end0, far_end1)
        for block, copies in zip(far, tile_copies()):
            for copy in copies:
                copy.wait_recv()
            out_copy(block).start()

    for q in quarters:
        part_sent(PARTNER, r, q)
        for j in (1, 2, 3):
            fit_copy(j, q).wait_send()
    for q in (0, 1):
        part_sent(MATE, r, q)

    @pl.when(is_inner)
    def _():
        for q in quarters:
            part_sent(FAR, r, q)
            part_sent(FAR, end0, q)
            part_sent(MATE, far_inner0, q)
            part_sent(MATE, far_end0, q)
            for j in (1, 2, 3):
                near_copy(j, q).wait_send()
        for copies in tile_copies():
            for copy in copies:
                copy.wait_send()

    @pl.when(is_end)
    def _():
        for q in quarters:
            part_sent(PARTNER, end1, q)
            part_sent(MATE, inner0, q)
            if q > 1:
                part_sent(MATE, r, q)
                part_sent(PARTNER, inner1, q)

    for block in range(Y_SIZE * Z_SIZE):
        out_copy(block).wait()


def per_device(factors):
    row_count, local_funcs, occupied = factors.shape
    groups = lax.axis_size("fit")
    blocks = lax.axis_size("row")
    if (groups, blocks) != (4, Y_SIZE * Z_SIZE):
        return gathered_by_collectives(factors)
    sub = row_count // groups
    width = local_funcs * occupied
    out_shape = jax.ShapeDtypeStruct((row_count, blocks * sub), jnp.float32)
    out = pl.pallas_call(
        kernel,
        out_shape=out_shape,
        in_specs=[pl.BlockSpec(memory_space=pl.ANY)],
        out_specs=pl.BlockSpec(memory_space=pl.ANY),
        scratch_shapes=[
            pltpu.VMEM((row_count, width), factors.dtype),
            pltpu.VMEM((row_count, blocks * sub), jnp.float32),
            pltpu.VMEM((groups - 1, row_count, width), factors.dtype),
            pltpu.VMEM((groups - 1, groups, sub, width), factors.dtype),
            pltpu.VMEM((blocks, groups, sub, width), factors.dtype),
            pltpu.VMEM((groups, groups, sub, sub), jnp.float32),
            pltpu.SemaphoreType.DMA((3, 4)),
            pltpu.SemaphoreType.DMA((3, 4)),
            pltpu.SemaphoreType.DMA((3, 4)),
            pltpu.SemaphoreType.DMA((3, 4)),
            pltpu.SemaphoreType.DMA((3, blocks, 8)),
            pltpu.SemaphoreType.DMA((blocks, 8)),
            pltpu.SemaphoreType.DMA((4, 8)),
            pltpu.SemaphoreType.DMA((4, 8)),
            pltpu.SemaphoreType.DMA((blocks,)),
            pltpu.SemaphoreType.DMA,
        ],
        compiler_params=pltpu.CompilerParams(
            collective_id=0, has_side_effects=True, vmem_limit_bytes=62 * 2**20
        ),
        cost_estimate=pl.CostEstimate(
            flops=2 * row_count * blocks * sub * groups * width,
            bytes_accessed=4 * row_count * blocks * sub,
            transcendentals=0,
        ),
    )(factors.reshape(row_count, width))
    return out.reshape(1, row_count, blocks * sub)


def solution(mesh):
    return jax.shard_map(
        per_device,
        mesh=mesh,
        in_specs=(P("row", "fit", None),),
        out_specs=P("fit", "row", None),
        check_vma=False,
    )
```
